512 devices in a mesh: row: 4 (over z_lo), col: 16 (over z_hi, y), depth: 8 (over x, core).
Axes of the slice: x: 4, y: 4, z: 16 (z_hi: 4, z_lo: 4; z = z_hi * 4 + z_lo), core: 2. Of those that a mesh axis runs over, the one named last changes fastest.
Arguments:
- activations: bfloat16 [8192, 4096], P(('depth', 'row'), 'col'), may hold values from -6 to 6
- gate_grad: bfloat16 [8192, 16384], P(('depth', 'col'), 'row'), may hold values from -6 to 6
- turn_lengths: int32 [64], replicated, may hold values from 1 to 256, 8192 in all
Outputs:
- weight_grad: bfloat16 [4096, 16384], P('col', ('row', 'depth'))
The draws below stay inside these ranges and needn't reach their ends.
Inputs may be any that keep to these rules, and one draw needn't show every extreme that they name: `turn_lengths`: the 64 lengths sum to 8192; the longest is exactly 256.
All inputs are finite; a program needn't handle non-finite values.
Results may differ from the reference program's by a relative error of at most 0.0043.
Values may be sent and summed in bfloat16 or wider, within the bound.
A program may use at most 64 MiB of HBM per device.

```python
import math
import jax
import jax.numpy as jnp
import numpy as np
from jax import lax

D = 4096
FF = 16384
TURNS = 64
TOKENS = 8192
MOST_LEN = 256


def levels(key, extent, split, least, high):
    def one(axis_at, shards_of):
        heights = jax.random.uniform(jax.random.fold_in(jax.random.fold_in(key, 6), axis_at), (shards_of,), jnp.float32, least / len(split), high / len(split))
        return jnp.repeat(jnp.exp(heights), extent[axis_at] // shards_of).reshape((-1,) + (1,) * (len(extent) - axis_at - 1))

    loudness = one(*split[0])
    for cut in split[1:]:
        loudness = loudness * one(*cut)
    return loudness


def split_up(number_of, total, limit, lean):
    weights = [(1 << 20) // math.isqrt(standing ** lean) + 1 for standing in range(2, number_of + 1)]
    rest, given = total - limit - (number_of - 1), [1] * (number_of - 1)
    while rest > 0:
        candidates = [i for i in range(number_of - 1) if given[i] < limit]
        pool, remaining = sum([weights[i] for i in candidates]), rest
        for i in candidates:
            more = min(limit - given[i], max(1, remaining * weights[i] // pool), rest)
            given[i] = given[i] + more
            rest = rest - more
    return np.array([limit] + given)


def ragged_sizes(key, count, total, bound, lean):
    if count == 2:
        one = jax.random.randint(key, (), max(1, total - bound), min(bound, total - 1) + 1)
        return jnp.stack([one, total - one])
    lengths = jnp.asarray(split_up(count, total, bound, lean), jnp.int32)
    couples = (count - 1) // 2
    source_of, sink = lengths[1:1 + 2 * couples:2], lengths[2:2 + 2 * couples:2]
    slack = jnp.minimum(source_of - 1, bound - sink)
    shifted = jax.random.randint(jax.random.fold_in(key, 1), (couples,), 0, 1 << 20) % (slack + 1)
    lengths = lengths.at[1:1 + 2 * couples:2].set(source_of - shifted).at[2:2 + 2 * couples:2].set(sink + shifted)
    return lengths[jax.random.permutation(jax.random.fold_in(key, 2), count)]


def scatter_about(own_key, dims, deviation, bound, pieces=(), kind=jnp.bfloat16):
    factor_of = levels(own_key, dims, pieces, -0.22, 0.18) if pieces else 1.0
    result = jax.random.normal(own_key, dims, jnp.float32) * deviation * factor_of
    return jnp.minimum(jnp.maximum(result, -bound), bound).astype(kind)


def setup_inputs(seed: int = 0) -> dict:
    splits = jax.random.split(jax.random.key(seed), 4)
    return {
        "activations": scatter_about(splits[0], (TOKENS, D), 1.0, 6.0, ((0, 32), (1, 16))),
        "gate_grad": scatter_about(splits[1], (TOKENS, FF), 1.0, 6.0, ((0, 128), (1, 4))),
        "turn_lengths": ragged_sizes(splits[2], TURNS, TOKENS, MOST_LEN, 2).astype(jnp.int32),
    }


def turn_weighting(gate_grad, turn_lengths):
    endings = jnp.cumsum(turn_lengths).astype(jnp.int32)
    begins = (endings - turn_lengths).astype(jnp.int32)
    token_pos = jnp.arange(gate_grad.shape[0], dtype=jnp.int32)
    inside = (token_pos[:, None] >= begins[None, :]) & (token_pos[:, None] < endings[None, :])
    turn_len = jnp.sum(jnp.where(inside, turn_lengths[None, :], 0), axis=1).astype(jnp.int32)
    return (gate_grad.astype(jnp.float32) / turn_len.astype(jnp.float32)[:, None]).astype(jnp.bfloat16)


def reference(activations, gate_grad, turn_lengths):
    weighted = turn_weighting(gate_grad, turn_lengths)
    totals = lax.dot_general(activations, weighted, (((0,), (0,)), ((), ())), preferred_element_type=jnp.float32)
    return totals.astype(jnp.bfloat16)
```

```python
import jax
import jax.numpy as jnp
from jax import lax
from jax.experimental import pallas as pl
from jax.experimental.pallas import tpu as pltpu
from jax.sharding import PartitionSpec as P

MESH = pl.DeviceIdType.MESH
BF16, F32 = jnp.bfloat16, jnp.float32
HALVES = 2


def kernel(lens_ref, a_ref, g_ref, out_ref, a_mine, w_mine, a_all, w_all, c_out, c_in,
           a_send, a_recv, x_send, x_recv, d_send, d_recv, y_send, y_recv, c_send, c_recv):
    zl = lax.axis_index("row")
    col = lax.axis_index("col")
    depth = lax.axis_index("depth")
    zh, y = lax.div(col, 4), lax.rem(col, 4)
    x, k = lax.div(depth, 2), lax.rem(depth, 2)
    tokens, width = g_ref.shape
    feats = a_ref.shape[1]
    share = width // 8
    half = share // HALVES
    other = 1 - k
    mine = lax.rem(zl + 4 - zh, 4)

    def at(zl_=zl, zh_=zh, y_=y, depth_=depth):
        return (zl_, zh_ * 4 + y_, depth_)

    def turn(value, by):
        return lax.rem(value + by + 4, 4)

    swapped = at(zl_=zh, zh_=zl)
    off_diagonal = zl != zh
    peers = [at(zl_=turn(zl, i)) for i in (1, 2, 3)]
    peers += [at(y_=turn(y, i)) for i in (1, 2, 3)]
    peers += [at(zh_=turn(zh, i)) for i in (1, 3)]
    peers += [at(depth_=lax.rem(depth + i, 8)) for i in range(1, 8)]

    barrier = pltpu.get_barrier_semaphore()
    for peer in peers:
        pl.semaphore_signal(barrier, inc=1, device_id=peer, device_id_type=MESH)

    @pl.when(off_diagonal)
    def _():
        pl.semaphore_signal(barrier, inc=1, device_id=swapped, device_id_type=MESH)

    a_mine[...] = a_ref[...].astype(F32).T.astype(BF16)
    turns = lens_ref.shape[1]
    row = lens_ref[...].astype(F32)
    down = lax.broadcasted_iota(jnp.int32, (turns, turns), 0)
    across = lax.broadcasted_iota(jnp.int32, (turns, turns), 1)
    column = jnp.sum(jnp.where(down == across, row, 0.0), axis=1, keepdims=True)
    endings = jnp.sum(jnp.where(down <= across, column, 0.0), axis=0, keepdims=True)
    begins = endings - row
    token = (lax.broadcasted_iota(jnp.int32, (tokens, turns), 0) + (depth * 16 + col) * tokens).astype(F32)
    inside = (token >= begins) & (token < endings)
    turn_len = jnp.sum(jnp.where(inside, row, 0.0), axis=1, keepdims=True)
    for h in range(HALVES):
        for s in range(8):
            begin = s * share + h * half
            w_mine[h, s] = (g_ref[:, begin:begin + half].astype(F32) / turn_len).astype(BF16)

    pl.semaphore_wait(barrier, jnp.where(off_diagonal, 16, 15))

    sent = []

    def send(src, dst, send_sem, recv_sem, device):
        copy = pltpu.make_async_remote_copy(
            src_ref=src, dst_ref=dst, send_sem=send_sem, recv_sem=recv_sem, device_id=device, device_id_type=MESH)
        copy.start()
        sent.append(copy)

    def arrived(dst, recv_sem):
        pltpu.make_async_remote_copy(
            src_ref=dst, dst_ref=dst, send_sem=a_send.at[0], recv_sem=recv_sem, device_id=peers[0],
            device_id_type=MESH).wait_recv()

    first = pltpu.make_async_remote_copy(
        src_ref=a_mine, dst_ref=a_all.at[lax.rem(zh + 4 - zl, 4), depth], send_sem=a_send.at[0],
        recv_sem=a_recv.at[lax.rem(zh + 4 - zl, 4)], device_id=swapped, device_id_type=MESH)
    stay = pltpu.make_async_copy(a_mine, a_all.at[0, depth], a_recv.at[0])

    @pl.when(off_diagonal)
    def _():
        first.start()

    @pl.when(zl == zh)
    def _():
        stay.start()

    for h in range(HALVES):
        w_keep = pltpu.make_async_copy(w_mine.at[h, depth], w_all.at[h, depth, y], d_recv.at[h, 0])
        w_keep.start()
        for i in (1, 2, 6, 7, 3, 5, 4):
            to = lax.rem(depth + i, 8)
            send(w_mine.at[h, to], w_all.at[h, depth, y], d_send.at[h, i], d_recv.at[h, 8 - i], at(depth_=to))

    def dealt(h):
        pltpu.make_async_copy(w_mine.at[h, depth], w_all.at[h, depth, y], d_recv.at[h, 0]).wait()
        for i in (1, 2, 6, 7, 3, 5, 4):
            s = lax.rem(depth + i, 8)
            arrived(w_all.at[h, s, y], d_recv.at[h, i])

    def gather_y(h):
        for i in (1, 3, 2):
            send(w_all.at[h, :, y], w_all.at[h, :, y], y_send.at[h, i], y_recv.at[h, 4 - i], at(y_=turn(y, i)))

    def gathered_y(h):
        for i in (1, 3, 2):
            part = w_all.at[h, :, turn(y, i)]
            arrived(part, y_recv.at[h, i])

    def spread_x(r):
        piece = a_all.at[r, depth]
        send(piece, piece, x_send.at[r, 0], x_recv.at[r, depth], at(depth_=2 * x + other))
        for n, i in ((1, 1), (2, 3), (3, 2)):
            send(piece, piece, x_send.at[r, n], x_recv.at[r, depth], at(depth_=2 * turn(x, i) + k))

    def forward(r):
        for n, i in ((1, 1), (2, 3), (3, 2)):
            s = 2 * turn(x, i) + k
            piece = a_all.at[r, s]
            arrived(piece, x_recv.at[r, s])
            send(piece, piece, x_send.at[r, 3 + n], x_recv.at[r, s], at(depth_=2 * x + other))

    def complete(r):
        for i in range(4):
            s = 2 * turn(x, i) + other
            arrived(a_all.at[r, s], x_recv.at[r, s])

    def own_first():
        arrived(a_all.at[mine, depth], a_recv.at[mine])
        piece = a_all.at[mine, depth]
        for i in (1, 3, 2):
            send(piece, piece, a_send.at[i], a_recv.at[mine], at(zl_=turn(zl, i)))

    def in_block(r):
        @pl.when(mine != r)
        def _():
            arrived(a_all.at[r, depth], a_recv.at[r])

    def product(r, h):
        total = jnp.dot(a_all[r, 0], w_all[h, 0].reshape(4 * tokens, half), preferred_element_type=F32)
        for s in range(1, 8):
            total += jnp.dot(a_all[r, s], w_all[h, s].reshape(4 * tokens, half), preferred_element_type=F32)
        return total

    up, down_ = at(zh_=turn(zh, 1)), at(zh_=turn(zh, 3))

    def pass_on(n, value, device):
        c_out[n] = value.astype(BF16)
        send(c_out.at[n], c_in.at[n], c_send.at[n], c_recv.at[n], device)

    def came(n):
        arrived(c_in.at[n], c_recv.at[n])
        return c_in[n].astype(F32)

    dealt(0)
    gather_y(0)
    own_first()
    dealt(1)
    gather_y(1)
    in_block(2)
    spread_x(2)
    in_block(3)
    spread_x(3)
    forward(2)
    in_block(1)
    spread_x(1)
    in_block(0)
    spread_x(0)
    complete(2)
    gathered_y(0)
    pass_on(0, product(2, 0), up)
    forward(3)
    complete(3)
    pass_on(3, product(3, 0), down_)
    gathered_y(1)
    pass_on(4, product(2, 1), down_)
    forward(1)
    complete(1)
    pass_on(1, product(1, 1), up)
    pass_on(2, product(1, 0) + came(0), up)
    pass_on(5, product(3, 1) + came(4), down_)
    forward(0)
    complete(0)
    out_ref[:, :half] = (product(0, 0) + came(3) + came(2)).astype(BF16)
    out_ref[:, half:] = (product(0, 1) + came(1) + came(5)).astype(BF16)
    for copy in sent:
        copy.wait_send()

    @pl.when(off_diagonal)
    def _():
        first.wait_send()


def local(activations, gate_grad, turn_lengths):
    tokens, feats = activations.shape
    rows, width = gate_grad.shape
    half = width // 8 // HALVES
    dma = pltpu.SemaphoreType.DMA
    vmem = pl.BlockSpec(memory_space=pltpu.VMEM)
    return pl.pallas_call(
        kernel,
        name="weight_grad",
        out_shape=jax.ShapeDtypeStruct((feats, width // 8), BF16),
        in_specs=[vmem] * 3,
        out_specs=vmem,
        scratch_shapes=[
            pltpu.VMEM((feats, tokens), BF16),
            pltpu.VMEM((HALVES, 8, rows, half), BF16),
            pltpu.VMEM((4, 8, feats, tokens), BF16),
            pltpu.VMEM((HALVES, 8, 4, rows, half), BF16),
            pltpu.VMEM((6, feats, half), BF16),
            pltpu.VMEM((6, feats, half), BF16),
            dma((4,)), dma((4,)),
            dma((4, 7)), dma((4, 8)),
            dma((HALVES, 8)), dma((HALVES, 8)),
            dma((HALVES, 4)), dma((HALVES, 4)),
            dma((6,)), dma((6,)),
        ],
        compiler_params=pltpu.CompilerParams(
            collective_id=0, has_side_effects=True, vmem_limit_bytes=48 * 2**20),
        cost_estimate=pl.CostEstimate(
            flops=2 * 4 * feats * 32 * rows * width // 8, bytes_accessed=2 * (tokens * feats + rows * width),
            transcendentals=0),
    )(turn_lengths.reshape(1, -1), activations, gate_grad)


def solution(mesh):
    in_specs = (P(("depth", "row"), "col"), P(("depth", "col"), "row"), P())
    out_specs = P("col", ("row", "depth"))
    return jax.shard_map(local, mesh=mesh, in_specs=in_specs, out_specs=out_specs, check_vma=False)
```

```python
import jax
import jax.numpy as jnp
from jax import lax
from jax.experimental import pallas as pl
from jax.experimental.pallas import tpu as pltpu
from jax.sharding import PartitionSpec as P

MESH = pl.DeviceIdType.MESH
BF16, F32 = jnp.bfloat16, jnp.float32
HALVES = 2


def kernel(lens_hbm, a_hbm, g_hbm, out_ref, lens_ref, a_ref, g_ref, a_mine, w_mine, a_all, w_all, c_out, c_in,
           in_sem, a_send, a_recv, x_send, x_recv, d_send, d_recv, y_send, y_recv, c_send, c_recv):
    zl = lax.axis_index("row")
    col = lax.axis_index("col")
    depth = lax.axis_index("depth")
    zh, y = lax.div(col, 4), lax.rem(col, 4)
    x, k = lax.div(depth, 2), lax.rem(depth, 2)
    tokens, width = g_ref.shape
    feats = a_ref.shape[1]
    some = feats // HALVES
    share = width // 8
    half = share // HALVES
    other = 1 - k
    mine = lax.rem(zl + 4 - zh, 4)
    theirs = lax.rem(zh + 4 - zl, 4)

    def at(zl_=zl, zh_=zh, y_=y, depth_=depth):
        return (zl_, zh_ * 4 + y_, depth_)

    def turn(value, by):
        return lax.rem(value + by + 4, 4)

    swapped = at(zl_=zh, zh_=zl)
    off_diagonal = zl != zh
    peers = [at(zl_=turn(zl, i)) for i in (1, 2, 3)]
    peers += [at(y_=turn(y, i)) for i in (1, 3)]
    peers += [at(zh_=turn(zh, i)) for i in (1, 3)]
    peers += [at(depth_=lax.rem(depth + i, 8)) for i in range(1, 8)]

    barrier = pltpu.get_barrier_semaphore()
    loads = [pltpu.make_async_copy(src, dst, in_sem.at[n])
             for n, (src, dst) in enumerate(((lens_hbm, lens_ref), (a_hbm, a_ref), (g_hbm, g_ref)))]
    for load in loads:
        load.start()
    for peer in peers:
        pl.semaphore_signal(barrier, inc=1, device_id=peer, device_id_type=MESH)

    @pl.when(off_diagonal)
    def _():
        pl.semaphore_signal(barrier, inc=1, device_id=swapped, device_id_type=MESH)

    loads[0].wait()
    turns = lens_ref.shape[1]
    row = lens_ref[...].astype(F32)
    down = lax.broadcasted_iota(jnp.int32, (turns, turns), 0)
    across = lax.broadcasted_iota(jnp.int32, (turns, turns), 1)
    column = jnp.sum(jnp.where(down == across, row, 0.0), axis=1, keepdims=True)
    endings = jnp.sum(jnp.where(down <= across, column, 0.0), axis=0, keepdims=True)
    begins = endings - row
    token = (lax.broadcasted_iota(jnp.int32, (tokens, turns), 0) + (depth * 16 + col) * tokens).astype(F32)
    inside = (token >= begins) & (token < endings)
    turn_len = jnp.sum(jnp.where(inside, row, 0.0), axis=1, keepdims=True)
    loads[1].wait()
    a_mine[...] = a_ref[...].astype(F32).T.astype(BF16)
    loads[2].wait()
    for h in range(HALVES):
        for s in range(8):
            begin = s * share + h * half
            w_mine[h, s] = (g_ref[:, begin:begin + half].astype(F32) / turn_len).astype(BF16)

    pl.semaphore_wait(barrier, jnp.where(off_diagonal, len(peers) + 1, len(peers)))

    sent = []

    def send(src, dst, send_sem, recv_sem, device):
        copy = pltpu.make_async_remote_copy(
            src_ref=src, dst_ref=dst, send_sem=send_sem, recv_sem=recv_sem, device_id=device, device_id_type=MESH)
        copy.start()
        sent.append(copy)

    def arrived(dst, recv_sem):
        pltpu.make_async_remote_copy(
            src_ref=dst, dst_ref=dst, send_sem=a_send.at[0, 0], recv_sem=recv_sem, device_id=peers[0],
            device_id_type=MESH).wait_recv()

    def part(r, s, e):
        return a_all.at[r, s, pl.ds(e * some, some)]

    first = []
    for e in range(HALVES):
        source = a_mine.at[pl.ds(e * some, some)]
        go = pltpu.make_async_remote_copy(
            src_ref=source, dst_ref=part(theirs, depth, e), send_sem=a_send.at[e, 0],
            recv_sem=a_recv.at[theirs, e], device_id=swapped, device_id_type=MESH)
        stay = pltpu.make_async_copy(source, part(0, depth, e), a_recv.at[0, e])
        first.append(go)
        pl.when(off_diagonal)(go.start)
        pl.when(zl == zh)(stay.start)

    for h in range(HALVES):
        pltpu.make_async_copy(w_mine.at[h, depth], w_all.at[h, depth, y], d_recv.at[h, 0]).start()
        for i in (1, 2, 6, 7, 3, 5, 4):
            to = lax.rem(depth + i, 8)
            send(w_mine.at[h, to], w_all.at[h, depth, y], d_send.at[h, i], d_recv.at[h, 8 - i], at(depth_=to))

    def dealt(h):
        pltpu.make_async_copy(w_mine.at[h, depth], w_all.at[h, depth, y], d_recv.at[h, 0]).wait()
        for i in (1, 2, 6, 7, 3, 5, 4):
            arrived(w_all.at[h, lax.rem(depth + i, 8), y], d_recv.at[h, i])
        whole = w_all.at[h, :, y]
        for n, i in ((0, 1), (1, 3)):
            send(whole, whole, y_send.at[h, n], y_recv.at[h, n], at(y_=turn(y, i)))

    def relay_y(h):
        for n, i, begin in ((0, 1, 0), (1, 3, 4)):
            back = turn(y, 4 - i)
            arrived(w_all.at[h, :, back], y_recv.at[h, n])
            four = w_all.at[h, pl.ds(begin, 4), back]
            send(four, four, y_send.at[h, 2 + n], y_recv.at[h, 2 + n], at(y_=turn(y, i)))

    def gathered_y(h):
        for n, begin in ((0, 0), (1, 4)):
            arrived(w_all.at[h, pl.ds(begin, 4), turn(y, 2)], y_recv.at[h, 2 + n])

    def own_first(e):
        piece = part(mine, depth, e)
        arrived(piece, a_recv.at[mine, e])
        for i in (1, 3, 2):
            send(piece, piece, a_send.at[e, i], a_recv.at[mine, e], at(zl_=turn(zl, i)))

    sibling = at(depth_=2 * x + other)

    def spread_x(r, e):
        piece = part(r, depth, e)

        @pl.when(mine != r)
        def _():
            arrived(piece, a_recv.at[r, e])

        for n, device in ((0, at(depth_=2 * turn(x, 1) + k)), (1, at(depth_=2 * turn(x, 3) + k)), (2, sibling)):
            send(piece, piece, x_send.at[r, e, n], x_recv.at[r, e, depth], device)

    def relay_x(r, e):
        for n, i in ((0, 3), (1, 1)):
            s = 2 * turn(x, i) + k
            piece = part(r, s, e)
            arrived(piece, x_recv.at[r, e, s])
            if n == e:
                send(piece, piece, x_send.at[r, e, 3], x_recv.at[r, e, s], at(depth_=2 * turn(x, 4 - i) + k))
            send(piece, piece, x_send.at[r, e, 4 + n], x_recv.at[r, e, s], sibling)

    def last_x(r, e):
        s = 2 * turn(x, 2) + k
        piece = part(r, s, e)
        arrived(piece, x_recv.at[r, e, s])
        send(piece, piece, x_send.at[r, e, 6], x_recv.at[r, e, s], sibling)

    def complete(r, e):
        for i in (0, 3, 1, 2):
            s = 2 * turn(x, i) + other
            arrived(part(r, s, e), x_recv.at[r, e, s])

    def product(r, e, h):
        total = None
        for s in range(8):
            term = jnp.dot(a_all[r, s, e * some:(e + 1) * some], w_all[h, s].reshape(4 * tokens, half),
                           preferred_element_type=F32)
            total = term if total is None else total + term
        return total

    up, below = at(zh_=turn(zh, 1)), at(zh_=turn(zh, 3))

    def pass_on(n, e, value, device):
        c_out[n, e] = value.astype(BF16)
        send(c_out.at[n, e], c_in.at[n, e], c_send.at[n, e], c_recv.at[n, e], device)

    def came(n, e):
        arrived(c_in.at[n, e], c_recv.at[n, e])
        return c_in[n, e].astype(F32)

    dealt(0)
    own_first(0)
    dealt(1)
    own_first(1)
    spread_x(2, 0)
    spread_x(3, 0)
    relay_y(0)
    relay_x(2, 0)
    relay_x(3, 0)
    spread_x(2, 1)
    spread_x(3, 1)
    last_x(2, 0)
    last_x(3, 0)
    gathered_y(0)
    complete(2, 0)
    pass_on(0, 0, product(2, 0, 0), up)
    complete(3, 0)
    pass_on(3, 0, product(3, 0, 0), below)
    relay_y(1)
    relay_x(2, 1)
    relay_x(3, 1)
    spread_x(1, 0)
    spread_x(1, 1)
    last_x(2, 1)
    last_x(3, 1)
    complete(2, 1)
    pass_on(0, 1, product(2, 1, 0), up)
    complete(3, 1)
    pass_on(3, 1, product(3, 1, 0), below)
    relay_x(1, 0)
    relay_x(1, 1)
    spread_x(0, 0)
    spread_x(0, 1)
    last_x(1, 0)
    last_x(1, 1)
    gathered_y(1)
    pass_on(4, 0, product(2, 0, 1), below)
    complete(1, 0)
    pass_on(1, 0, product(1, 0, 1), up)
    pass_on(4, 1, product(2, 1, 1), below)
    complete(1, 1)
    pass_on(1, 1, product(1, 1, 1), up)
    relay_x(0, 0)
    relay_x(0, 1)
    last_x(0, 0)
    last_x(0, 1)
    for e in range(HALVES):
        pass_on(2, e, product(1, e, 0) + came(0, e), up)
        pass_on(5, e, product(3, e, 1) + came(4, e), below)
    for e in range(HALVES):
        complete(0, e)
    for e in range(HALVES):
        rows = slice(e * some, (e + 1) * some)
        out_ref[rows, :half] = (product(0, e, 0) + came(3, e) + came(2, e)).astype(BF16)
        out_ref[rows, half:] = (product(0, e, 1) + came(1, e) + came(5, e)).astype(BF16)
    for copy in sent:
        copy.wait_send()
    for go in first:
        pl.when(off_diagonal)(go.wait_send)


def local(activations, gate_grad, turn_lengths):
    tokens, feats = activations.shape
    rows, width = gate_grad.shape
    half = width // 8 // HALVES
    dma = pltpu.SemaphoreType.DMA
    return pl.pallas_call(
        kernel,
        name="weight_grad",
        out_shape=jax.ShapeDtypeStruct((feats, width // 8), BF16),
        in_specs=[pl.BlockSpec(memory_space=pl.ANY)] * 3,
        out_specs=pl.BlockSpec(memory_space=pltpu.VMEM),
        scratch_shapes=[
            pltpu.VMEM((1, turn_lengths.shape[0]), jnp.int32),
            pltpu.VMEM((tokens, feats), BF16),
            pltpu.VMEM((rows, width), BF16),
            pltpu.VMEM((feats, tokens), BF16),
            pltpu.VMEM((HALVES, 8, rows, half), BF16),
            pltpu.VMEM((4, 8, feats, tokens), BF16),
            pltpu.VMEM((HALVES, 8, 4, rows, half), BF16),
            pltpu.VMEM((6, HALVES, feats // HALVES, half), BF16),
            pltpu.VMEM((6, HALVES, feats // HALVES, half), BF16),
            dma((3,)),
            dma((HALVES, 4)), dma((4, HALVES)),
            dma((4, HALVES, 7)), dma((4, HALVES, 8)),
            dma((HALVES, 8)), dma((HALVES, 8)),
            dma((HALVES, 4)), dma((HALVES, 4)),
            dma((6, HALVES)), dma((6, HALVES)),
        ],
        compiler_params=pltpu.CompilerParams(
            collective_id=0, has_side_effects=True, vmem_limit_bytes=60 * 2**20),
        cost_estimate=pl.CostEstimate(
            flops=2 * 4 * feats * 32 * rows * width // 8, bytes_accessed=2 * (tokens * feats + rows * width),
            transcendentals=0),
    )(turn_lengths.reshape(1, -1), activations, gate_grad)


def solution(mesh):
    in_specs = (P(("depth", "row"), "col"), P(("depth", "col"), "row"), P())
    out_specs = P("col", ("row", "depth"))
    return jax.shard_map(local, mesh=mesh, in_specs=in_specs, out_specs=out_specs, check_vma=False)
```

```python
import jax
import jax.numpy as jnp
from jax import lax
from jax.experimental import pallas as pl
from jax.experimental.pallas import tpu as pltpu
from jax.sharding import PartitionSpec as P

MESH = pl.DeviceIdType.MESH
BF16, F32 = jnp.bfloat16, jnp.float32
FEATS = ((0, 128), (128, 128))
HALVES = 2


def kernel(lens_hbm, a_hbm, g_hbm, out_ref, lens_ref, a_ref, g_ref, a_mine, w_mine, a_all, w_all, c_out, c_in,
           in_sem, a_send, a_recv, x_send, x_recv, d_send, d_recv, y_send, y_recv, c_send, c_recv):
    zl = lax.axis_index("row")
    col = lax.axis_index("col")
    depth = lax.axis_index("depth")
    zh, y = lax.div(col, 4), lax.rem(col, 4)
    x, k = lax.div(depth, 2), lax.rem(depth, 2)
    tokens, width = g_ref.shape
    feats = a_ref.shape[1]
    share = width // 8
    half = share // HALVES
    other = 1 - k

    def slot(piece, block):
        first = jnp.where(piece == 0, 0, lax.rem(piece, 3) + 1)
        fourth = jnp.where(piece == 3, 3, lax.rem(piece + 2, 3))
        return jnp.where(block == 0, first, jnp.where(block == 3, fourth, piece))

    def from_slot(place, block):
        return sum(jnp.where(slot(jnp.int32(piece), block) == place, piece, 0) for piece in range(4))

    source_zh = from_slot(zl, zh)
    mine = lax.rem(source_zh + 4 - zh, 4)
    theirs = lax.rem(zh + 4 - zl, 4)

    def at(zl_=zl, zh_=zh, y_=y, depth_=depth):
        return (zl_, zh_ * 4 + y_, depth_)

    def turn(value, by):
        return lax.rem(value + by + 4, 4)

    target = at(zl_=slot(zh, zl), zh_=zl)
    origin = at(zl_=zh, zh_=source_zh)
    off_diagonal = zl != zh
    comes = source_zh != zh
    peers = [at(zl_=turn(zl, i)) for i in (1, 2, 3)]
    peers += [at(y_=turn(y, i)) for i in (1, 3)]
    peers += [at(zh_=turn(zh, i)) for i in (1, 3)]
    peers += [at(depth_=lax.rem(depth + i, 8)) for i in range(1, 8)]

    barrier = pltpu.get_barrier_semaphore()
    loads = [pltpu.make_async_copy(src, dst, in_sem.at[n])
             for n, (src, dst) in enumerate(((a_hbm, a_ref), (lens_hbm, lens_ref), (g_hbm, g_ref)))]
    for load in loads:
        load.start()
    for peer in peers:
        pl.semaphore_signal(barrier, inc=1, device_id=peer, device_id_type=MESH)

    @pl.when(comes)
    def _():
        pl.semaphore_signal(barrier, inc=1, device_id=origin, device_id_type=MESH)

    loads[0].wait()
    a_mine[...] = a_ref[...].astype(F32).T.astype(BF16)

    pl.semaphore_wait(barrier, jnp.where(off_diagonal, len(peers) + 1, len(peers)))

    sent = []

    def send(src, dst, send_sem, recv_sem, device):
        copy = pltpu.make_async_remote_copy(
            src_ref=src, dst_ref=dst, send_sem=send_sem, recv_sem=recv_sem, device_id=device, device_id_type=MESH)
        copy.start()
        sent.append(copy)

    def arrived(dst, recv_sem):
        pltpu.make_async_remote_copy(
            src_ref=dst, dst_ref=dst, send_sem=a_send.at[0, 0], recv_sem=recv_sem, device_id=peers[0],
            device_id_type=MESH).wait_recv()

    def part(r, s, e):
        return a_all.at[r, s, pl.ds(*FEATS[e])]

    first = []
    for e in range(len(FEATS)):
        source = a_mine.at[pl.ds(*FEATS[e])]
        go = pltpu.make_async_remote_copy(
            src_ref=source, dst_ref=part(theirs, depth, e), send_sem=a_send.at[e, 0],
            recv_sem=a_recv.at[theirs, e], device_id=target, device_id_type=MESH)
        stay = pltpu.make_async_copy(source, part(0, depth, e), a_recv.at[0, e])
        first.append(go)
        pl.when(off_diagonal)(go.start)
        pl.when(zl == zh)(stay.start)

    loads[1].wait()
    turns = lens_ref.shape[1]
    row = lens_ref[...].astype(F32)
    down = lax.broadcasted_iota(jnp.int32, (turns, turns), 0)
    across = lax.broadcasted_iota(jnp.int32, (turns, turns), 1)
    column = jnp.sum(jnp.where(down == across, row, 0.0), axis=1, keepdims=True)
    endings = jnp.sum(jnp.where(down <= across, column, 0.0), axis=0, keepdims=True)
    begins = endings - row
    token = (lax.broadcasted_iota(jnp.int32, (tokens, turns), 0) + (depth * 16 + col) * tokens).astype(F32)
    inside = (token >= begins) & (token < endings)
    turn_len = jnp.sum(jnp.where(inside, row, 0.0), axis=1, keepdims=True)
    loads[2].wait()
    for h in range(HALVES):
        for s in range(8):
            begin = s * share + h * half
            w_mine[h, s] = (g_ref[:, begin:begin + half].astype(F32) / turn_len).astype(BF16)

    for h in range(HALVES):
        pltpu.make_async_copy(w_mine.at[h, depth], w_all.at[h, depth, y], d_recv.at[h, 0]).start()
        for i in (1, 2, 6, 7, 3, 5, 4):
            to = lax.rem(depth + i, 8)
            send(w_mine.at[h, to], w_all.at[h, depth, y], d_send.at[h, i], d_recv.at[h, 8 - i], at(depth_=to))

    def dealt(h):
        pltpu.make_async_copy(w_mine.at[h, depth], w_all.at[h, depth, y], d_recv.at[h, 0]).wait()
        for i in (1, 2, 6, 7, 3, 5, 4):
            arrived(w_all.at[h, lax.rem(depth + i, 8), y], d_recv.at[h, i])
        whole = w_all.at[h, :, y]
        for n, i in ((0, 1), (1, 3)):
            send(whole, whole, y_send.at[h, n], y_recv.at[h, n], at(y_=turn(y, i)))

    def relay_y(h):
        for n, i, begin in ((0, 1, 0), (1, 3, 4)):
            back = turn(y, 4 - i)
            arrived(w_all.at[h, :, back], y_recv.at[h, n])
            four = w_all.at[h, pl.ds(begin, 4), back]
            send(four, four, y_send.at[h, 2 + n], y_recv.at[h, 2 + n], at(y_=turn(y, i)))

    def gathered_y(h):
        for n, begin in ((0, 0), (1, 4)):
            arrived(w_all.at[h, pl.ds(begin, 4), turn(y, 2)], y_recv.at[h, 2 + n])

    def own_first(e):
        piece = part(mine, depth, e)
        arrived(piece, a_recv.at[mine, e])
        for i in (1, 3, 2):
            send(piece, piece, a_send.at[e, i], a_recv.at[mine, e], at(zl_=turn(zl, i)))

    sibling = at(depth_=2 * x + other)

    def spread_x(r, e):
        piece = part(r, depth, e)

        @pl.when(mine != r)
        def _():
            arrived(piece, a_recv.at[r, e])

        for n, i in enumerate((1, 3, 2)):
            send(piece, piece, x_send.at[r, e, n], x_recv.at[r, e, depth], at(depth_=2 * turn(x, i) + k))
        send(piece, piece, x_send.at[r, e, 3], x_recv.at[r, e, depth], sibling)

    def relay_x(r, e):
        for n, i in enumerate((1, 3, 2)):
            s = 2 * turn(x, i) + k
            piece = part(r, s, e)
            arrived(piece, x_recv.at[r, e, s])
            send(piece, piece, x_send.at[r, e, 4 + n], x_recv.at[r, e, s], sibling)

    def complete(r, e):
        for i in (0, 3, 1, 2):
            s = 2 * turn(x, i) + other
            arrived(part(r, s, e), x_recv.at[r, e, s])

    def product(r, e, h):
        total = None
        begin, size = FEATS[e]
        for s in range(8):
            term = jnp.dot(a_all[r, s, begin:begin + size], w_all[h, s].reshape(4 * tokens, half),
                           preferred_element_type=F32)
            total = term if total is None else total + term
        return total

    up, below = at(zh_=turn(zh, 1)), at(zh_=turn(zh, 3))

    def pass_on(n, h, value, device):
        c_out[n, h] = value.astype(BF16)
        send(c_out.at[n, h], c_in.at[n, h], c_send.at[n, h], c_recv.at[n, h], device)

    def came(n, h):
        arrived(c_in.at[n, h], c_recv.at[n, h])
        return c_in[n, h].astype(F32)

    dealt(0)
    own_first(0)
    own_first(1)
    spread_x(2, 0)
    spread_x(3, 0)
    relay_y(0)
    dealt(1)
    relay_x(2, 0)
    relay_x(3, 0)
    spread_x(1, 1)
    spread_x(2, 1)
    spread_x(1, 0)
    spread_x(3, 1)
    gathered_y(0)
    complete(2, 0)
    pass_on(0, 0, product(2, 0, 0), up)
    complete(3, 0)
    pass_on(4, 0, product(3, 0, 0), below)
    relay_x(1, 1)
    relay_x(2, 1)
    relay_y(1)
    complete(2, 1)
    pass_on(3, 0, product(2, 1, 0), below)
    complete(1, 1)
    pass_on(1, 0, product(1, 1, 0), up)
    relay_x(1, 0)
    relay_x(3, 1)
    gathered_y(1)
    pass_on(0, 1, product(2, 0, 1), up)
    pass_on(4, 1, product(3, 0, 1), below)
    pass_on(1, 1, product(1, 1, 1), up)
    pass_on(3, 1, product(2, 1, 1), below)
    spread_x(0, 0)
    spread_x(0, 1)
    complete(1, 0)
    pass_on(2, 0, product(1, 0, 0) + came(0, 0), up)
    pass_on(2, 1, product(1, 0, 1) + came(0, 1), up)
    complete(3, 1)
    pass_on(5, 0, product(3, 1, 0) + came(3, 0), below)
    pass_on(5, 1, product(3, 1, 1) + came(3, 1), below)
    relay_x(0, 0)
    relay_x(0, 1)
    for e in range(len(FEATS)):
        complete(0, e)
    for h in range(HALVES):
        units = pl.ds(h * half, half)
        out_ref[pl.ds(*FEATS[0]), units] = (product(0, 0, h) + came(4, h) + came(2, h)).astype(BF16)
        out_ref[pl.ds(*FEATS[1]), units] = (product(0, 1, h) + came(1, h) + came(5, h)).astype(BF16)
    for copy in sent:
        copy.wait_send()
    for go in first:
        pl.when(off_diagonal)(go.wait_send)


def local(activations, gate_grad, turn_lengths):
    tokens, feats = activations.shape
    rows, width = gate_grad.shape
    share = width // 8
    half = share // 2
    f = len(FEATS)
    dma = pltpu.SemaphoreType.DMA
    return pl.pallas_call(
        kernel,
        name="weight_grad",
        out_shape=jax.ShapeDtypeStruct((feats, width // 8), BF16),
        in_specs=[pl.BlockSpec(memory_space=pl.ANY)] * 3,
        out_specs=pl.BlockSpec(memory_space=pltpu.VMEM),
        scratch_shapes=[
            pltpu.VMEM((1, turn_lengths.shape[0]), jnp.int32),
            pltpu.VMEM((tokens, feats), BF16),
            pltpu.VMEM((rows, width), BF16),
            pltpu.VMEM((feats, tokens), BF16),
            pltpu.VMEM((HALVES, 8, rows, share // HALVES), BF16),
            pltpu.VMEM((4, 8, feats, tokens), BF16),
            pltpu.VMEM((HALVES, 8, 4, rows, share // HALVES), BF16),
            pltpu.VMEM((6, HALVES, feats // 2, half), BF16),
            pltpu.VMEM((6, HALVES, feats // 2, half), BF16),
            dma((3,)),
            dma((f, 4)), dma((4, f)),
            dma((4, f, 7)), dma((4, f, 8)),
            dma((HALVES, 8)), dma((HALVES, 8)),
            dma((HALVES, 4)), dma((HALVES, 4)),
            dma((6, HALVES)), dma((6, HALVES)),
        ],
        compiler_params=pltpu.CompilerParams(
            collective_id=0, has_side_effects=True, vmem_limit_bytes=60 * 2**20),
        cost_estimate=pl.CostEstimate(
            flops=2 * 4 * feats * 32 * rows * width // 8, bytes_accessed=2 * (tokens * feats + rows * width),
            transcendentals=0),
    )(turn_lengths.reshape(1, -1), activations, gate_grad)


def solution(mesh):
    in_specs = (P(("depth", "row"), "col"), P(("depth", "col"), "row"), P())
    out_specs = P("col", ("row", "depth"))
    return jax.shard_map(local, mesh=mesh, in_specs=in_specs, out_specs=out_specs, check_vma=False)
```

```python
import jax
import jax.numpy as jnp
from jax import lax
from jax.experimental import pallas as pl
from jax.experimental.pallas import tpu as pltpu
from jax.sharding import PartitionSpec as P

MESH = pl.DeviceIdType.MESH
BF16, F32 = jnp.bfloat16, jnp.float32
FEATS = ((0, 128), (128, 128))
HALVES = 2


def kernel(lens_hbm, a_hbm, g_hbm, out_ref, lens_ref, a_ref, g_ref, a_mine, w_mine, a_all, w_all, c_out, c_in, total,
           in_sem, a_send, a_recv, x_send, x_recv, d_send, d_recv, y_send, y_recv, c_send, c_recv):
    zl = lax.axis_index("row")
    col = lax.axis_index("col")
    depth = lax.axis_index("depth")
    zh, y = lax.div(col, 4), lax.rem(col, 4)
    x, k = lax.div(depth, 2), lax.rem(depth, 2)
    tokens, width = g_ref.shape
    feats = a_ref.shape[1]
    share = width // 8
    half = share // HALVES
    other = 1 - k

    def slot(piece, block):
        first = jnp.where(piece == 0, 0, lax.rem(piece, 3) + 1)
        fourth = jnp.where(piece == 3, 3, lax.rem(piece + 2, 3))
        return jnp.where(block == 0, first, jnp.where(block == 3, fourth, piece))

    def from_slot(place, block):
        return sum(jnp.where(slot(jnp.int32(piece), block) == place, piece, 0) for piece in range(4))

    source_zh = from_slot(zl, zh)
    mine = lax.rem(source_zh + 4 - zh, 4)
    theirs = lax.rem(zh + 4 - zl, 4)

    def at(zl_=zl, zh_=zh, y_=y, depth_=depth):
        return (zl_, zh_ * 4 + y_, depth_)

    def turn(value, by):
        return lax.rem(value + by + 4, 4)

    target = at(zl_=slot(zh, zl), zh_=zl)
    origin = at(zl_=zh, zh_=source_zh)
    off_diagonal = zl != zh
    comes = source_zh != zh
    peers = [at(zl_=turn(zl, i)) for i in (1, 2, 3)]
    peers += [at(y_=turn(y, i)) for i in (1, 3)]
    peers += [at(zh_=turn(zh, i)) for i in (1, 3)]
    peers += [at(depth_=lax.rem(depth + i, 8)) for i in range(1, 8)]

    barrier = pltpu.get_barrier_semaphore()
    loads = [pltpu.make_async_copy(src, dst, in_sem.at[n])
             for n, (src, dst) in enumerate(((a_hbm, a_ref), (lens_hbm, lens_ref), (g_hbm, g_ref)))]
    for load in loads:
        load.start()
    for peer in peers:
        pl.semaphore_signal(barrier, inc=1, device_id=peer, device_id_type=MESH)

    @pl.when(comes)
    def _():
        pl.semaphore_signal(barrier, inc=1, device_id=origin, device_id_type=MESH)

    loads[0].wait()
    a_mine[...] = a_ref[...].astype(F32).T.astype(BF16)

    pl.semaphore_wait(barrier, jnp.where(off_diagonal, len(peers) + 1, len(peers)))

    sent = []

    def send(src, dst, send_sem, recv_sem, device):
        copy = pltpu.make_async_remote_copy(
            src_ref=src, dst_ref=dst, send_sem=send_sem, recv_sem=recv_sem, device_id=device, device_id_type=MESH)
        copy.start()
        sent.append(copy)

    def arrived(dst, recv_sem):
        pltpu.make_async_remote_copy(
            src_ref=dst, dst_ref=dst, send_sem=a_send.at[0, 0], recv_sem=recv_sem, device_id=peers[0],
            device_id_type=MESH).wait_recv()

    def part(r, s, e):
        return a_all.at[r, s, pl.ds(*FEATS[e])]

    first = []
    for e in range(len(FEATS)):
        source = a_mine.at[pl.ds(*FEATS[e])]
        go = pltpu.make_async_remote_copy(
            src_ref=source, dst_ref=part(theirs, depth, e), send_sem=a_send.at[e, 0],
            recv_sem=a_recv.at[theirs, e], device_id=target, device_id_type=MESH)
        stay = pltpu.make_async_copy(source, part(0, depth, e), a_recv.at[0, e])
        first.append(go)
        pl.when(off_diagonal)(go.start)
        pl.when(zl == zh)(stay.start)

    loads[1].wait()
    turns = lens_ref.shape[1]
    row = lens_ref[...].astype(F32)
    down = lax.broadcasted_iota(jnp.int32, (turns, turns), 0)
    across = lax.broadcasted_iota(jnp.int32, (turns, turns), 1)
    column = jnp.sum(jnp.where(down == across, row, 0.0), axis=1, keepdims=True)
    endings = jnp.sum(jnp.where(down <= across, column, 0.0), axis=0, keepdims=True)
    begins = endings - row
    token = (lax.broadcasted_iota(jnp.int32, (tokens, turns), 0) + (depth * 16 + col) * tokens).astype(F32)
    inside = (token >= begins) & (token < endings)
    turn_len = jnp.sum(jnp.where(inside, row, 0.0), axis=1, keepdims=True)
    loads[2].wait()
    for h in range(HALVES):
        for s in range(8):
            begin = s * share + h * half
            w_mine[h, s] = (g_ref[:, begin:begin + half].astype(F32) / turn_len).astype(BF16)

    for h in range(HALVES):
        pltpu.make_async_copy(w_mine.at[h, depth], w_all.at[h, depth, y], d_recv.at[h, 0]).start()
        for i in (1, 2, 6, 7, 3, 5, 4):
            to = lax.rem(depth + i, 8)
            send(w_mine.at[h, to], w_all.at[h, depth, y], d_send.at[h, i], d_recv.at[h, 8 - i], at(depth_=to))

    def dealt(h):
        pltpu.make_async_copy(w_mine.at[h, depth], w_all.at[h, depth, y], d_recv.at[h, 0]).wait()
        for i in (1, 2, 6, 7, 3, 5, 4):
            arrived(w_all.at[h, lax.rem(depth + i, 8), y], d_recv.at[h, i])
        whole = w_all.at[h, :, y]
        for n, i in ((0, 1), (1, 3)):
            send(whole, whole, y_send.at[h, n], y_recv.at[h, n], at(y_=turn(y, i)))

    def relay_y(h):
        for n, i, begin in ((0, 1, 0), (1, 3, 4)):
            back = turn(y, 4 - i)
            arrived(w_all.at[h, :, back], y_recv.at[h, n])
            four = w_all.at[h, pl.ds(begin, 4), back]
            send(four, four, y_send.at[h, 2 + n], y_recv.at[h, 2 + n], at(y_=turn(y, i)))

    def gathered_y(h):
        for n, begin in ((0, 0), (1, 4)):
            arrived(w_all.at[h, pl.ds(begin, 4), turn(y, 2)], y_recv.at[h, 2 + n])

    def own_first(e):
        piece = part(mine, depth, e)
        arrived(piece, a_recv.at[mine, e])
        for i in (1, 3, 2):
            send(piece, piece, a_send.at[e, i], a_recv.at[mine, e], at(zl_=turn(zl, i)))

    sibling = at(depth_=2 * x + other)

    def spread_x(r, e):
        piece = part(r, depth, e)

        @pl.when(mine != r)
        def _():
            arrived(piece, a_recv.at[r, e])

        for n, i in enumerate((1, 3, 2)):
            send(piece, piece, x_send.at[r, e, n], x_recv.at[r, e, depth], at(depth_=2 * turn(x, i) + k))
        send(piece, piece, x_send.at[r, e, 3], x_recv.at[r, e, depth], sibling)

    def relay_x(r, e):
        for n, i in enumerate((1, 3, 2)):
            s = 2 * turn(x, i) + k
            piece = part(r, s, e)
            arrived(piece, x_recv.at[r, e, s])
            send(piece, piece, x_send.at[r, e, 4 + n], x_recv.at[r, e, s], sibling)

    def complete(r, e):
        for i in (0, 3, 1, 2):
            s = 2 * turn(x, i) + other
            arrived(part(r, s, e), x_recv.at[r, e, s])

    def product(r, e, h):
        total = None
        begin, size = FEATS[e]
        for s in range(8):
            term = jnp.dot(a_all[r, s, begin:begin + size], w_all[h, s].reshape(4 * tokens, half),
                           preferred_element_type=F32)
            total = term if total is None else total + term
        return total

    up, below = at(zh_=turn(zh, 1)), at(zh_=turn(zh, 3))

    def pass_on(n, h, value, device):
        c_out[n, h] = value.astype(BF16)
        send(c_out.at[n, h], c_in.at[n, h], c_send.at[n, h], c_recv.at[n, h], device)

    def came(n, h):
        arrived(c_in.at[n, h], c_recv.at[n, h])
        return c_in[n, h].astype(F32)

    def two_away_last():
        c_out[3, 1] = product(2, 1, 1).astype(BF16)
        into = jnp.where(zh == 1, 6, 3)
        send(c_out.at[3, 1], c_in.at[into, 1], c_send.at[3, 1], c_recv.at[into, 1],
             at(zh_=turn(zh, jnp.where(zh == 1, 1, 3))))

    def straight_up_last():
        value = product(1, 1, 1)

        @pl.when(zh == 2)
        def _():
            c_out[1, 1] = (value + came(6, 1)).astype(BF16)

        @pl.when(zh != 2)
        def _():
            c_out[1, 1] = value.astype(BF16)

        send(c_out.at[1, 1], c_in.at[1, 1], c_send.at[1, 1], c_recv.at[1, 1], up)

    def pass_down_last():
        value = product(3, 1, 1)

        @pl.when(zh != 0)
        def _():
            c_out[5, 1] = (value + came(3, 1)).astype(BF16)

        @pl.when(zh == 0)
        def _():
            c_out[5, 1] = value.astype(BF16)

        send(c_out.at[5, 1], c_in.at[5, 1], c_send.at[5, 1], c_recv.at[5, 1], below)

    dealt(0)
    own_first(0)
    own_first(1)
    spread_x(2, 0)
    spread_x(3, 0)
    relay_y(0)
    dealt(1)
    relay_x(2, 0)
    relay_x(3, 0)
    spread_x(1, 1)
    spread_x(2, 1)
    spread_x(1, 0)
    spread_x(3, 1)
    gathered_y(0)
    complete(2, 0)
    pass_on(0, 0, product(2, 0, 0), up)
    complete(3, 0)
    pass_on(4, 0, product(3, 0, 0), below)
    relay_x(1, 1)
    relay_x(2, 1)
    relay_y(1)
    complete(2, 1)
    pass_on(3, 0, product(2, 1, 0), below)
    complete(1, 1)
    pass_on(1, 0, product(1, 1, 0), up)
    relay_x(1, 0)
    relay_x(3, 1)
    gathered_y(1)
    pass_on(0, 1, product(2, 0, 1), up)
    pass_on(4, 1, product(3, 0, 1), below)
    two_away_last()
    spread_x(0, 0)
    spread_x(0, 1)
    complete(1, 0)
    pass_on(2, 0, product(1, 0, 0) + came(0, 0), up)
    straight_up_last()
    pass_on(2, 1, product(1, 0, 1) + came(0, 1), up)
    complete(3, 1)
    pass_on(5, 0, product(3, 1, 0) + came(3, 0), below)
    pass_down_last()
    relay_x(0, 0)
    relay_x(0, 1)
    for e in range(len(FEATS)):
        complete(0, e)
    for e, early in ((0, 4), (1, 1)):
        for h in range(HALVES):
            total[pl.ds(*FEATS[e]), pl.ds(h * half, half)] = product(0, e, h) + came(early, h)
    for h in range(HALVES):
        for e, late in ((0, 2), (1, 5)):
            rows, units = pl.ds(*FEATS[e]), pl.ds(h * half, half)
            out_ref[rows, units] = (total[rows, units] + came(late, h)).astype(BF16)
    for copy in sent:
        copy.wait_send()
    for go in first:
        pl.when(off_diagonal)(go.wait_send)


def local(activations, gate_grad, turn_lengths):
    tokens, feats = activations.shape
    rows, width = gate_grad.shape
    share = width // 8
    half = share // 2
    f = len(FEATS)
    dma = pltpu.SemaphoreType.DMA
    return pl.pallas_call(
        kernel,
        name="weight_grad",
        out_shape=jax.ShapeDtypeStruct((feats, width // 8), BF16),
        in_specs=[pl.BlockSpec(memory_space=pl.ANY)] * 3,
        out_specs=pl.BlockSpec(memory_space=pltpu.VMEM),
        scratch_shapes=[
            pltpu.VMEM((1, turn_lengths.shape[0]), jnp.int32),
            pltpu.VMEM((tokens, feats), BF16),
            pltpu.VMEM((rows, width), BF16),
            pltpu.VMEM((feats, tokens), BF16),
            pltpu.VMEM((HALVES, 8, rows, share // HALVES), BF16),
            pltpu.VMEM((4, 8, feats, tokens), BF16),
            pltpu.VMEM((HALVES, 8, 4, rows, share // HALVES), BF16),
            pltpu.VMEM((6, HALVES, feats // 2, half), BF16),
            pltpu.VMEM((7, HALVES, feats // 2, half), BF16),
            pltpu.VMEM((feats, share), F32),
            dma((3,)),
            dma((f, 4)), dma((4, f)),
            dma((4, f, 7)), dma((4, f, 8)),
            dma((HALVES, 8)), dma((HALVES, 8)),
            dma((HALVES, 4)), dma((HALVES, 4)),
            dma((6, HALVES)), dma((7, HALVES)),
        ],
        compiler_params=pltpu.CompilerParams(
            collective_id=0, has_side_effects=True, vmem_limit_bytes=60 * 2**20),
        cost_estimate=pl.CostEstimate(
            flops=2 * 4 * feats * 32 * rows * width // 8, bytes_accessed=2 * (tokens * feats + rows * width),
            transcendentals=0),
    )(turn_lengths.reshape(1, -1), activations, gate_grad)


def solution(mesh):
    in_specs = (P(("depth", "row"), "col"), P(("depth", "col"), "row"), P())
    out_specs = P("col", ("row", "depth"))
    return jax.shard_map(local, mesh=mesh, in_specs=in_specs, out_specs=out_specs, check_vma=False)
```

```python
import jax
import jax.numpy as jnp
from jax import lax
from jax.experimental import pallas as pl
from jax.experimental.pallas import tpu as pltpu
from jax.sharding import PartitionSpec as P

MESH = pl.DeviceIdType.MESH
BF16, F32 = jnp.bfloat16, jnp.float32
FEATS = ((0, 128), (128, 128))
HALVES = 2


def kernel(lens_hbm, a_hbm, g_hbm, out_ref, lens_ref, a_ref, g_ref, a_mine, w_mine, a_all, w_all, c_out, c_in, total,
           in_sem, a_send, a_recv, x_send, x_recv, d_send, d_recv, y_send, y_recv, c_send, c_recv):
    zl = lax.axis_index("row")
    col = lax.axis_index("col")
    depth = lax.axis_index("depth")
    zh, y = lax.div(col, 4), lax.rem(col, 4)
    x, k = lax.div(depth, 2), lax.rem(depth, 2)
    tokens, width = g_ref.shape
    feats = a_ref.shape[1]
    share = width // 8
    half = share // HALVES
    other = 1 - k

    def slot(piece, block):
        first = jnp.where(piece == 0, 0, lax.rem(piece, 3) + 1)
        fourth = jnp.where(piece == 3, 3, lax.rem(piece + 2, 3))
        return jnp.where(block == 0, first, jnp.where(block == 3, fourth, piece))

    def from_slot(place, block):
        return sum(jnp.where(slot(jnp.int32(piece), block) == place, piece, 0) for piece in range(4))

    source_zh = from_slot(zl, zh)
    mine = lax.rem(source_zh + 4 - zh, 4)
    theirs = lax.rem(zh + 4 - zl, 4)

    def at(zl_=zl, zh_=zh, y_=y, depth_=depth):
        return (zl_, zh_ * 4 + y_, depth_)

    def turn(value, by):
        return lax.rem(value + by + 4, 4)

    target = at(zl_=slot(zh, zl), zh_=zl)
    origin = at(zl_=zh, zh_=source_zh)
    off_diagonal = zl != zh
    comes = source_zh != zh
    peers = [at(zl_=turn(zl, i)) for i in (1, 2, 3)]
    peers += [at(y_=turn(y, i)) for i in (1, 3)]
    peers += [at(zh_=turn(zh, i)) for i in (1, 3)]
    peers += [at(depth_=lax.rem(depth + i, 8)) for i in range(1, 8)]

    barrier = pltpu.get_barrier_semaphore()
    loads = [pltpu.make_async_copy(src, dst, in_sem.at[n])
             for n, (src, dst) in enumerate(((a_hbm, a_ref), (lens_hbm, lens_ref), (g_hbm, g_ref)))]
    for load in loads:
        load.start()
    for peer in peers:
        pl.semaphore_signal(barrier, inc=1, device_id=peer, device_id_type=MESH)

    @pl.when(comes)
    def _():
        pl.semaphore_signal(barrier, inc=1, device_id=origin, device_id_type=MESH)

    loads[0].wait()
    a_mine[...] = a_ref[...].astype(F32).T.astype(BF16)

    pl.semaphore_wait(barrier, jnp.where(off_diagonal, len(peers) + 1, len(peers)))

    sent = []

    def send(src, dst, send_sem, recv_sem, device):
        copy = pltpu.make_async_remote_copy(
            src_ref=src, dst_ref=dst, send_sem=send_sem, recv_sem=recv_sem, device_id=device, device_id_type=MESH)
        copy.start()
        sent.append(copy)

    def arrived(dst, recv_sem):
        pltpu.make_async_remote_copy(
            src_ref=dst, dst_ref=dst, send_sem=a_send.at[0, 0], recv_sem=recv_sem, device_id=peers[0],
            device_id_type=MESH).wait_recv()

    def part(r, s, e):
        return a_all.at[r, s, pl.ds(*FEATS[e])]

    first = []
    for e in range(len(FEATS)):
        source = a_mine.at[pl.ds(*FEATS[e])]
        go = pltpu.make_async_remote_copy(
            src_ref=source, dst_ref=part(theirs, depth, e), send_sem=a_send.at[e, 0],
            recv_sem=a_recv.at[theirs, e], device_id=target, device_id_type=MESH)
        stay = pltpu.make_async_copy(source, part(0, depth, e), a_recv.at[0, e])
        first.append(go)
        pl.when(off_diagonal)(go.start)
        pl.when(zl == zh)(stay.start)

    loads[1].wait()
    turns = lens_ref.shape[1]
    row = lens_ref[...].astype(F32)
    down = lax.broadcasted_iota(jnp.int32, (turns, turns), 0)
    across = lax.broadcasted_iota(jnp.int32, (turns, turns), 1)
    column = jnp.sum(jnp.where(down == across, row, 0.0), axis=1, keepdims=True)
    endings = jnp.sum(jnp.where(down <= across, column, 0.0), axis=0, keepdims=True)
    begins = endings - row
    token = (lax.broadcasted_iota(jnp.int32, (tokens, turns), 0) + (depth * 16 + col) * tokens).astype(F32)
    inside = (token >= begins) & (token < endings)
    turn_len = jnp.sum(jnp.where(inside, row, 0.0), axis=1, keepdims=True)
    loads[2].wait()
    for h in range(HALVES):
        for s in range(8):
            begin = s * share + h * half
            w_mine[h, s] = (g_ref[:, begin:begin + half].astype(F32) / turn_len).astype(BF16)

    for h in range(HALVES):
        pltpu.make_async_copy(w_mine.at[h, depth], w_all.at[h, depth, y], d_recv.at[h, 0]).start()
        for i in (1, 2, 6, 7, 3, 5, 4):
            to = lax.rem(depth + i, 8)
            send(w_mine.at[h, to], w_all.at[h, depth, y], d_send.at[h, i], d_recv.at[h, 8 - i], at(depth_=to))

    def dealt(h):
        pltpu.make_async_copy(w_mine.at[h, depth], w_all.at[h, depth, y], d_recv.at[h, 0]).wait()
        for i in (1, 2, 6, 7, 3, 5, 4):
            arrived(w_all.at[h, lax.rem(depth + i, 8), y], d_recv.at[h, i])
        whole = w_all.at[h, :, y]
        for n, i in ((0, 1), (1, 3)):
            send(whole, whole, y_send.at[h, n], y_recv.at[h, n], at(y_=turn(y, i)))

    def relay_y(h):
        for n, i, begin in ((0, 1, 0), (1, 3, 4)):
            back = turn(y, 4 - i)
            arrived(w_all.at[h, :, back], y_recv.at[h, n])
            four = w_all.at[h, pl.ds(begin, 4), back]
            send(four, four, y_send.at[h, 2 + n], y_recv.at[h, 2 + n], at(y_=turn(y, i)))

    def gathered_y(h):
        for n, begin in ((0, 0), (1, 4)):
            arrived(w_all.at[h, pl.ds(begin, 4), turn(y, 2)], y_recv.at[h, 2 + n])

    def own_first(e):
        piece = part(mine, depth, e)
        arrived(piece, a_recv.at[mine, e])
        for i in (1, 3, 2):
            send(piece, piece, a_send.at[e, i], a_recv.at[mine, e], at(zl_=turn(zl, i)))

    sibling = at(depth_=2 * x + other)

    def spread_x(r, e):
        piece = part(r, depth, e)

        @pl.when(mine != r)
        def _():
            arrived(piece, a_recv.at[r, e])

        for n, i in enumerate((1, 3, 2)):
            send(piece, piece, x_send.at[r, e, n], x_recv.at[r, e, depth], at(depth_=2 * turn(x, i) + k))
        send(piece, piece, x_send.at[r, e, 3], x_recv.at[r, e, depth], sibling)

    def relay_x(r, e):
        for n, i in enumerate((1, 3, 2)):
            s = 2 * turn(x, i) + k
            piece = part(r, s, e)
            arrived(piece, x_recv.at[r, e, s])
            send(piece, piece, x_send.at[r, e, 4 + n], x_recv.at[r, e, s], sibling)

    def complete(r, e):
        for i in (0, 3, 1, 2):
            s = 2 * turn(x, i) + other
            arrived(part(r, s, e), x_recv.at[r, e, s])

    def product(r, e, h):
        total = None
        begin, size = FEATS[e]
        for s in range(8):
            term = jnp.dot(a_all[r, s, begin:begin + size], w_all[h, s].reshape(4 * tokens, half),
                           preferred_element_type=F32)
            total = term if total is None else total + term
        return total

    up, below = at(zh_=turn(zh, 1)), at(zh_=turn(zh, 3))

    def pass_on(n, h, value, device):
        c_out[n, h] = value.astype(BF16)
        send(c_out.at[n, h], c_in.at[n, h], c_send.at[n, h], c_recv.at[n, h], device)

    def came(n, h):
        arrived(c_in.at[n, h], c_recv.at[n, h])
        return c_in[n, h].astype(F32)

    def two_away_last():
        c_out[3, 1] = product(2, 1, 1).astype(BF16)
        into = jnp.where(zh == 1, 6, 3)
        send(c_out.at[3, 1], c_in.at[into, 1], c_send.at[3, 1], c_recv.at[into, 1],
             at(zh_=turn(zh, jnp.where(zh == 1, 1, 3))))

    def straight_up_last():
        value = product(1, 1, 1)

        @pl.when(zh == 2)
        def _():
            c_out[1, 1] = (value + came(6, 1)).astype(BF16)

        @pl.when(zh != 2)
        def _():
            c_out[1, 1] = value.astype(BF16)

        send(c_out.at[1, 1], c_in.at[1, 1], c_send.at[1, 1], c_recv.at[1, 1], up)

    def pass_down_last():
        value = product(3, 1, 1)

        @pl.when(zh != 0)
        def _():
            c_out[5, 1] = (value + came(3, 1)).astype(BF16)

        @pl.when(zh == 0)
        def _():
            c_out[5, 1] = value.astype(BF16)

        send(c_out.at[5, 1], c_in.at[5, 1], c_send.at[5, 1], c_recv.at[5, 1], below)

    dealt(0)
    own_first(0)
    own_first(1)
    spread_x(2, 0)
    spread_x(3, 0)
    relay_y(0)
    dealt(1)
    relay_x(2, 0)
    relay_x(3, 0)
    spread_x(1, 1)
    spread_x(2, 1)
    spread_x(1, 0)
    spread_x(3, 1)
    gathered_y(0)
    complete(2, 0)
    pass_on(0, 0, product(2, 0, 0), up)
    complete(3, 0)
    pass_on(4, 0, product(3, 0, 0), below)
    relay_x(1, 1)
    relay_x(2, 1)
    relay_y(1)
    complete(2, 1)
    pass_on(3, 0, product(2, 1, 0), below)
    complete(1, 1)
    pass_on(1, 0, product(1, 1, 0), up)
    relay_x(1, 0)
    relay_x(3, 1)
    spread_x(0, 0)
    spread_x(0, 1)
    gathered_y(1)
    two_away_last()
    pass_on(0, 1, product(2, 0, 1), up)
    pass_on(4, 1, product(3, 0, 1), below)
    complete(1, 0)
    pass_on(2, 0, product(1, 0, 0) + came(0, 0), up)
    straight_up_last()
    pass_on(2, 1, product(1, 0, 1) + came(0, 1), up)
    complete(3, 1)
    pass_on(5, 0, product(3, 1, 0) + came(3, 0), below)
    pass_down_last()
    relay_x(0, 0)
    relay_x(0, 1)
    for e in range(len(FEATS)):
        complete(0, e)
    for e, early in ((0, 4), (1, 1)):
        for h in range(HALVES):
            total[pl.ds(*FEATS[e]), pl.ds(h * half, half)] = product(0, e, h) + came(early, h)
    for h in range(HALVES):
        for e, late in ((0, 2), (1, 5)):
            rows, units = pl.ds(*FEATS[e]), pl.ds(h * half, half)
            out_ref[rows, units] = (total[rows, units] + came(late, h)).astype(BF16)
    for copy in sent:
        copy.wait_send()
    for go in first:
        pl.when(off_diagonal)(go.wait_send)


def local(activations, gate_grad, turn_lengths):
    tokens, feats = activations.shape
    rows, width = gate_grad.shape
    share = width // 8
    half = share // 2
    f = len(FEATS)
    dma = pltpu.SemaphoreType.DMA
    return pl.pallas_call(
        kernel,
        name="weight_grad",
        out_shape=jax.ShapeDtypeStruct((feats, width // 8), BF16),
        in_specs=[pl.BlockSpec(memory_space=pl.ANY)] * 3,
        out_specs=pl.BlockSpec(memory_space=pltpu.VMEM),
        scratch_shapes=[
            pltpu.VMEM((1, turn_lengths.shape[0]), jnp.int32),
            pltpu.VMEM((tokens, feats), BF16),
            pltpu.VMEM((rows, width), BF16),
            pltpu.VMEM((feats, tokens), BF16),
            pltpu.VMEM((HALVES, 8, rows, share // HALVES), BF16),
            pltpu.VMEM((4, 8, feats, tokens), BF16),
            pltpu.VMEM((HALVES, 8, 4, rows, share // HALVES), BF16),
            pltpu.VMEM((6, HALVES, feats // 2, half), BF16),
            pltpu.VMEM((7, HALVES, feats // 2, half), BF16),
            pltpu.VMEM((feats, share), F32),
            dma((3,)),
            dma((f, 4)), dma((4, f)),
            dma((4, f, 7)), dma((4, f, 8)),
            dma((HALVES, 8)), dma((HALVES, 8)),
            dma((HALVES, 4)), dma((HALVES, 4)),
            dma((6, HALVES)), dma((7, HALVES)),
        ],
        compiler_params=pltpu.CompilerParams(
            collective_id=0, has_side_effects=True, vmem_limit_bytes=60 * 2**20),
        cost_estimate=pl.CostEstimate(
            flops=2 * 4 * feats * 32 * rows * width // 8, bytes_accessed=2 * (tokens * feats + rows * width),
            transcendentals=0),
    )(turn_lengths.reshape(1, -1), activations, gate_grad)


def solution(mesh):
    in_specs = (P(("depth", "row"), "col"), P(("depth", "col"), "row"), P())
    out_specs = P("col", ("row", "depth"))
    return jax.shard_map(local, mesh=mesh, in_specs=in_specs, out_specs=out_specs, check_vma=False)
```
